32 devices in a mesh: chan: 8 (over z, x), tm: 4 (over y, core).
Axes of the slice: x: 2, y: 2, z: 4, core: 2. Of those that a mesh axis runs over, the one named last changes fastest.
Arguments:
- voltages: bfloat16 [2, 2, 8, 2048, 2048], P(None, None, None, 'chan', 'tm'), may hold values from -6 to 6
- weights: bfloat16 [8, 2, 2, 32, 2048], P('chan'), may hold values from -0.09375 to 0.09375
- channel_map: int32 [8], replicated, may hold values from 0 to 7, each once
- sweep_response_taps: float32 [8, 2, 32, 256], P('chan', None, 'tm'), may hold values from -6 to 6
- chirp_length: int32 [32], P('tm'), may hold values from 32 to 256, as said below
Outputs:
- dedispersed: float32 [8, 2, 2, 32, 2048], P('chan', None, None, 'tm')
The draws below stay inside these ranges and needn't reach their ends.
Inputs may be any that keep to these rules, and one draw needn't show every extreme that they name: `channel_map`: each channel appears once. `chirp_length`: one beam has the longest chirp of exactly 256 samples.
All inputs are finite; a program needn't handle non-finite values.
Results may differ from the reference program's by a relative error of at most 0.0003.
Values may be sent and summed in bfloat16 or wider, within the bound.
A program may use at most 128 MiB of HBM per device.

```python
import jax
import jax.numpy as jnp
from jax import lax

ANTENNA_COUNT = 2048
POLARISATION_NUM = 2
BEAM_COUNT = 32
LMAX = 256
CHANNEL_COUNT = 8
TIME_SAMPLES = 2048


def draw_chirp_length(key, part):
    lowest = max(2, LMAX // 8)
    base = jax.random.randint(jax.random.fold_in(key, 11), (BEAM_COUNT,), lowest, LMAX // 2 + 1)
    chosen = jax.random.randint(jax.random.fold_in(key, 12), (), 0, BEAM_COUNT)
    marker = jnp.arange(BEAM_COUNT, dtype=jnp.int32) == chosen
    return jnp.where(marker, LMAX, base).astype(jnp.int32)


def level_of(stream_key, dims, cuts, low, largest):
    factor_of, own = 1.0, jax.random.fold_in(stream_key, 6)
    for axis_at, blocks in cuts:
        draws = jnp.exp(jax.random.uniform(jax.random.fold_in(own, axis_at), (blocks,), jnp.float32, low / len(cuts), largest / len(cuts)))
        factor_of = factor_of * jnp.repeat(draws, dims[axis_at] // blocks).reshape([-1 if axis == axis_at else 1 for axis in range(len(dims))])
    return factor_of


def normal_values(stream_key, shape, spread, limit, pieces=(), kind=jnp.bfloat16):
    values = spread * jax.random.normal(stream_key, shape, jnp.float32)
    if pieces:
        values = values * level_of(stream_key, shape, pieces, -0.22, 0.18)
    return jnp.clip(values, -limit, limit).astype(kind)


def setup_inputs(seed: int = 0) -> dict:
    splits = jax.random.split(jax.random.key(seed), 6)
    voltages = normal_values(splits[0], (2, POLARISATION_NUM, CHANNEL_COUNT, ANTENNA_COUNT, TIME_SAMPLES), 1.0, 6.0, ((3, 8), (4, 4)))
    weights = normal_values(splits[1], (CHANNEL_COUNT, 2, POLARISATION_NUM, BEAM_COUNT, ANTENNA_COUNT), (2 * ANTENNA_COUNT) ** -0.5, 0.09375, ((0, 8),))
    channel_map = jax.random.permutation(splits[2], CHANNEL_COUNT).astype(jnp.int32)
    sweep_response_taps = normal_values(splits[3], (CHANNEL_COUNT, 2, BEAM_COUNT, LMAX), 1.0, 6.0, ((0, 8), (2, 4)), jnp.float32)
    chirp_length = draw_chirp_length(jax.random.fold_in(splits[5], 71), 0)
    return dict(voltages=voltages, weights=weights, channel_map=channel_map, sweep_response_taps=sweep_response_taps, chirp_length=chirp_length)


def reference(voltages, weights, channel_map, sweep_response_taps, chirp_length):
    longest = sweep_response_taps.shape[3]
    total = voltages.shape[4]
    lag = jnp.arange(longest, dtype=jnp.int32)
    inside = lag[None, :] < chirp_length.astype(jnp.int32)[:, None]
    factor = 1.0 / jnp.sqrt(chirp_length.astype(jnp.float32))[:, None]
    high = lax.Precision.HIGHEST

    def one_slot(slot):
        channel = channel_map[slot].astype(jnp.int32)
        volts = lax.dynamic_index_in_dim(voltages, channel, 2, keepdims=False).astype(jnp.float32)
        weight = lax.dynamic_index_in_dim(weights, slot, 0, keepdims=False).astype(jnp.float32)
        taps = lax.dynamic_index_in_dim(sweep_response_taps, slot, 0, keepdims=False)
        beam_real = jnp.einsum('pba,pat->pbt', weight[0], volts[0], precision=high) - jnp.einsum('pba,pat->pbt', weight[1], volts[1], precision=high)
        beam_imag = jnp.einsum('pba,pat->pbt', weight[0], volts[1], precision=high) + jnp.einsum('pba,pat->pbt', weight[1], volts[0], precision=high)
        resp_real = jnp.where(inside, taps[0], 0.0) * factor
        resp_imag = jnp.where(inside, taps[1], 0.0) * factor
        series = beam_real + 1j * beam_imag
        answer = resp_real + 1j * resp_imag
        extent = total + longest
        spectrum = jnp.fft.fft(series, n=extent, axis=-1) * jnp.fft.fft(answer, n=extent, axis=-1)[None]
        result = jnp.fft.ifft(spectrum, axis=-1)[..., :total]
        return jnp.stack([jnp.real(result), jnp.imag(result)], 0).astype(volts.dtype)
    return lax.map(one_slot, jnp.arange(channel_map.shape[0], dtype=jnp.int32))
```

```python
import functools
import math

import jax
import jax.numpy as jnp
import ml_dtypes
import numpy as np
from jax import lax
from jax.experimental import pallas as pl
from jax.experimental.pallas import tpu as pltpu
from jax.sharding import PartitionSpec as P

TOP = 32767.0
MESH = pl.DeviceIdType.MESH


def dot(left, right):
    return jnp.dot(left, right, preferred_element_type=jnp.float32)


def fourier_tables(extent):
    counter = np.arange(extent, dtype=np.int64)
    angle = (counter[:, None] * counter[None, :] % extent) * (2.0 * math.pi / extent)
    tables = []
    for table in (np.cos(angle), np.sin(angle)):
        high = table.astype(ml_dtypes.bfloat16)
        low = (table - high.astype(np.float64)).astype(ml_dtypes.bfloat16)
        tables += [high, low]
    return np.stack(tables)


def beam_kernel(groups, map_ref, volt_ref, weight_ref, code_ref, step_ref):
    pols, beams = weight_ref.shape[2], weight_ref.shape[3]
    reals, imags = [], []
    for p in range(pols):
        mixed = jnp.concatenate([weight_ref[0, 0, p], weight_ref[0, 1, p]], axis=0)
        left = dot(mixed, volt_ref[0, p, 0])
        right = dot(mixed, volt_ref[1, p, 0])
        reals.append(left[:beams] - right[beams:])
        imags.append(left[beams:] + right[:beams])
    share = beams // groups
    for g in range(groups):
        rows = jnp.concatenate([part[g * share : (g + 1) * share] for part in reals + imags], axis=0)
        peak = jnp.maximum(jnp.max(jnp.abs(rows), axis=0, keepdims=True), 1e-30)
        codes = jnp.round(rows * (TOP / peak)).astype(jnp.int32)
        code_ref[0, g] = codes.astype(jnp.int16)
        step_ref[0, g] = peak * (1.0 / TOP)


def form_beams(voltages, weights, channel_map, groups):
    parts, pols, channels, antennas, times = voltages.shape
    slots, beams = weights.shape[0], weights.shape[3]
    rows = 2 * pols * beams // groups
    return pl.pallas_call(
        functools.partial(beam_kernel, groups),
        grid_spec=pltpu.PrefetchScalarGridSpec(
            num_scalar_prefetch=1,
            grid=(slots,),
            in_specs=[
                pl.BlockSpec((parts, pols, 1, antennas, times), lambda j, m: (0, 0, m[j], 0, 0)),
                pl.BlockSpec((1, 2, pols, beams, antennas), lambda j, m: (j, 0, 0, 0, 0)),
            ],
            out_specs=[
                pl.BlockSpec((1, groups, rows, times), lambda j, m: (j, 0, 0, 0)),
                pl.BlockSpec((1, groups, 1, times), lambda j, m: (j, 0, 0, 0)),
            ],
        ),
        out_shape=[
            jax.ShapeDtypeStruct((slots, groups, rows, times), jnp.int16),
            jax.ShapeDtypeStruct((slots, groups, 1, times), jnp.float32),
        ],
        compiler_params=pltpu.CompilerParams(vmem_limit_bytes=24 << 20),
        name="form_beams",
    )(channel_map, voltages, weights)


def exchange_kernel(chans, groups, code_ref, step_ref, code_out, step_out, send, recv, own):
    chan, group = lax.axis_index("chan"), lax.axis_index("tm")
    total = chans * groups
    me = chan * groups + group
    barrier = pltpu.get_barrier_semaphore()

    def place(k):
        other = lax.rem(me + k, total)
        return other, (lax.div(other, groups), lax.rem(other, groups))

    @pl.loop(1, total)
    def _(k):
        pl.semaphore_signal(barrier, inc=1, device_id=place(k)[1], device_id_type=MESH)

    mine = [
        pltpu.make_async_copy(code_ref.at[me], code_out.at[me], own.at[0]),
        pltpu.make_async_copy(step_ref.at[me], step_out.at[me], own.at[1]),
    ]
    for copy in mine:
        copy.start()
    pl.semaphore_wait(barrier, total - 1)

    def copies(source, target, slot, device):
        return [
            pltpu.make_async_remote_copy(
                src_ref=a.at[source], dst_ref=b.at[target], send_sem=send.at[n, slot],
                recv_sem=recv.at[n, target], device_id=device, device_id_type=MESH,
            )
            for n, (a, b) in enumerate(((code_ref, code_out), (step_ref, step_out)))
        ]

    @pl.loop(1, total)
    def _(k):
        other, device = place(k)
        for copy in copies(other, me, k, device):
            copy.start()

    @pl.loop(1, total)
    def _(k):
        other, device = place(k)
        for copy in copies(other, other, k, device):
            copy.wait_send()
            copy.wait_recv()

    for copy in mine:
        copy.wait()


def exchange(codes, steps, chans, groups):
    total = chans * groups
    return pl.pallas_call(
        functools.partial(exchange_kernel, chans, groups),
        in_specs=[pl.BlockSpec(memory_space=pl.ANY)] * 2,
        out_specs=[pl.BlockSpec(memory_space=pl.ANY)] * 2,
        out_shape=[jax.ShapeDtypeStruct(a.shape, a.dtype) for a in (codes, steps)],
        scratch_shapes=[
            pltpu.SemaphoreType.DMA((2, total)),
            pltpu.SemaphoreType.DMA((2, total)),
            pltpu.SemaphoreType.DMA((2,)),
        ],
        compiler_params=pltpu.CompilerParams(collective_id=0, has_side_effects=True),
        name="exchange",
    )(codes, steps)


def split(value):
    high = value.astype(jnp.bfloat16)
    return high, (value - high.astype(jnp.float32)).astype(jnp.bfloat16)


def transform(value, high, low):
    rows = value.shape[0]
    first, second = split(value)
    both = dot(jnp.concatenate([first, second], axis=0), high)
    return both[:rows] + both[rows:] + dot(first, low)


def dedisperse_kernel(chans, groups, code_ref, step_ref, resp_ref, table_ref, out_ref, sums):
    longest, beams = resp_ref.shape[2], resp_ref.shape[1]
    rows, times = code_ref.shape[1], code_ref.shape[2]
    half = rows // 2
    for g in range(groups):

        def add(c, total, g=g):
            at = c * groups + g
            return total + code_ref[at].astype(jnp.int32).astype(jnp.float32) * step_ref[at]

        sums[g] = lax.fori_loop(0, chans, add, jnp.zeros((rows, times), jnp.float32))
    cos_high, cos_low, sin_high, sin_low = (table_ref[n] for n in range(4))
    resp = jnp.concatenate([resp_ref[0], resp_ref[1]], axis=0)
    by_cos = transform(resp, cos_high[:longest], cos_low[:longest])
    by_sin = transform(resp, sin_high[:longest], sin_low[:longest])
    gain_real = (by_cos[:beams] + by_sin[beams:])[None]
    gain_imag = (by_cos[beams:] - by_sin[:beams])[None]

    per = times // longest
    count = groups * per
    blocks = []
    for r in range(2):
        pieces = [jnp.zeros((half, longest), jnp.float32)]
        for m in range(count):
            pieces.append(sums[m // per, r * half : (r + 1) * half, (m % per) * longest : (m % per + 1) * longest])
        blocks += [jnp.concatenate([pieces[m], pieces[m + 1]], axis=1) for m in range(count)]
    stacked = jnp.concatenate(blocks, axis=0)
    size = count * half
    by_cos = transform(stacked, cos_high, cos_low)
    by_sin = transform(stacked, sin_high, sin_low)
    shape = (size // beams, beams, 2 * longest)
    spec_real = (by_cos[:size] + by_sin[size:]).reshape(shape)
    spec_imag = (by_cos[size:] - by_sin[:size]).reshape(shape)
    prod_real = (spec_real * gain_real - spec_imag * gain_imag).reshape(size, 2 * longest)
    prod_imag = (spec_real * gain_imag + spec_imag * gain_real).reshape(size, 2 * longest)
    stacked = jnp.concatenate([prod_real, prod_imag], axis=0) * (0.5 / longest)
    by_cos = transform(stacked, cos_high[:, longest:], cos_low[:, longest:])
    by_sin = transform(stacked, sin_high[:, longest:], sin_low[:, longest:])
    results = (by_cos[:size] - by_sin[size:], by_cos[size:] + by_sin[:size])
    for r in range(2):
        for m in range(count):
            for p in range(half // beams):
                start = m * half + p * beams
                out_ref[0, r, p, :, m * longest : (m + 1) * longest] = results[r][start : start + beams]


def dedisperse(codes, steps, resp, chans, groups):
    rows, times = codes.shape[1:]
    beams, longest = resp.shape[1:]
    return pl.pallas_call(
        functools.partial(dedisperse_kernel, chans, groups),
        in_specs=[pl.BlockSpec(memory_space=pltpu.VMEM)] * 4,
        out_specs=pl.BlockSpec(memory_space=pltpu.VMEM),
        out_shape=jax.ShapeDtypeStruct((1, 2, rows // (2 * beams), beams, groups * times), jnp.float32),
        scratch_shapes=[pltpu.VMEM((groups, rows, times), jnp.float32)],
        compiler_params=pltpu.CompilerParams(vmem_limit_bytes=40 << 20),
        name="dedisperse",
    )(codes, steps, resp, jnp.asarray(fourier_tables(2 * longest)))


def on_device(chans, groups, voltages, weights, channel_map, sweep_response_taps, chirp_length):
    parts, pols, beams, antennas = weights.shape[1:]
    longest = sweep_response_taps.shape[3]
    pieces = weights[0].reshape(parts, pols, beams, chans, antennas // chans).transpose(3, 0, 1, 2, 4)
    pieces = lax.all_to_all(pieces, "chan", split_axis=0, concat_axis=0, tiled=True)
    lag = jnp.arange(longest, dtype=jnp.int32)
    inside = lag[None, :] < chirp_length[:, None]
    factor = lax.rsqrt(chirp_length.astype(jnp.float32))[:, None]
    resp = jnp.where(inside, sweep_response_taps[0], 0.0) * factor
    codes, steps = form_beams(voltages, pieces, channel_map, groups)
    total = chans * groups
    codes, steps = exchange(codes.reshape((total,) + codes.shape[2:]), steps.reshape((total,) + steps.shape[2:]), chans, groups)
    return dedisperse(codes, steps, resp, chans, groups)


def solution(mesh):
    return jax.shard_map(
        functools.partial(on_device, mesh.shape["chan"], mesh.shape["tm"]),
        mesh=mesh,
        in_specs=(
            P(None, None, None, "chan", "tm"),
            P("chan", None, None, None, None),
            P(),
            P("chan", None, "tm", None),
            P("tm"),
        ),
        out_specs=P("chan", None, None, "tm", None),
        check_vma=False,
    )
```

```python
import functools
import math

import jax
import jax.numpy as jnp
import ml_dtypes
import numpy as np
from jax import lax
from jax.experimental import pallas as pl
from jax.experimental.pallas import tpu as pltpu
from jax.sharding import PartitionSpec as P

TOP = 32767.0
MESH = pl.DeviceIdType.MESH


def dot(left, right):
    return jnp.dot(left, right, preferred_element_type=jnp.float32)


def fourier_tables(extent):
    counter = np.arange(extent, dtype=np.int64)
    angle = (counter[:, None] * counter[None, :] % extent) * (2.0 * math.pi / extent)
    tables = []
    for table in (np.cos(angle), np.sin(angle)):
        high = table.astype(ml_dtypes.bfloat16)
        low = (table - high.astype(np.float64)).astype(ml_dtypes.bfloat16)
        tables += [high, low]
    return np.stack(tables)


def encode(rows):
    peak = jnp.maximum(jnp.max(jnp.abs(rows), axis=0, keepdims=True), 1e-30)
    codes = jnp.round(rows * (TOP / peak)).astype(jnp.int32).astype(jnp.int16)
    return codes, peak * (1.0 / TOP)


def decode(codes, step):
    return codes.astype(jnp.int32).astype(jnp.float32) * step


def form_kernel(
    chans, groups, sliced, map_ref, volt_ref, weight_ref, code_out, step_out,
    volts, mixes, away_code, away_step, near_code, near_step, sum_code, sum_step,
    own, weight_send, weight_recv, pass_send, pass_recv, near_send, near_recv, sum_send, sum_recv,
):
    pols, beams, antennas = mixes.shape[0], mixes.shape[3], mixes.shape[4]
    chan, group = lax.axis_index("chan"), lax.axis_index("tm")
    far, side = lax.div(chan, 2), lax.rem(chan, 2)
    fars = chans // 2
    half = lax.rem(group, 2)
    sibling = (chan, group + 1 - 2 * half)
    partner = (chan + 1 - 2 * side, group)
    total = chans * groups
    me = chan * groups + group
    barrier = pltpu.get_barrier_semaphore()

    @pl.loop(1, total)
    def _(k):
        other = lax.rem(me + k, total)
        device = (lax.div(other, groups), lax.rem(other, groups))
        pl.semaphore_signal(barrier, inc=1, device_id=device, device_id_type=MESH)

    def piece(p, target):
        if sliced:
            return weight_ref.at[:, p, :, pl.ds(pl.multiple_of(target * antennas, antennas), antennas)]
        return weight_ref.at[target, :, p]

    mine = [pltpu.make_async_copy(piece(p, chan), mixes.at[p, chan], own.at[p]) for p in range(pols)]
    load = pltpu.make_async_copy(volt_ref, volts, own.at[pols])
    pl.semaphore_wait(barrier, total - 1)

    def remote(source, target, send, recv, device):
        return pltpu.make_async_remote_copy(
            src_ref=source, dst_ref=target, send_sem=send, recv_sem=recv, device_id=device, device_id_type=MESH
        )

    def weight_copy(target, slot):
        return remote(piece(half, target), mixes.at[half, slot], weight_send.at[target], weight_recv.at[slot], (target, group))

    def pass_copy(p, slot):
        return remote(mixes.at[p, slot], mixes.at[p, slot], pass_send.at[slot], pass_recv.at[slot], sibling)

    @pl.loop(1, chans)
    def _(k):
        weight_copy(lax.rem(chan + k, chans), chan).start()

    for copy in mine:
        copy.start()
    load.start()
    for copy in mine:
        copy.wait()

    def far_of(i):
        return lax.rem(far + i + 1, fars)

    def pass_on(slot):
        @pl.when(slot != chan)
        def _():
            weight_copy(slot, slot).wait_recv()
            pass_copy(half, slot).start()

    @pl.loop(0, fars)
    def _(i):
        pass_on(2 * far_of(i) + 1 - side)

    load.wait()

    def partial(slot):
        @pl.when(slot != chan)
        def _():
            pass_copy(1 - half, slot).wait_recv()

        channel = map_ref[slot]
        reals, imags = [], []
        for p in range(pols):
            mixed = jnp.concatenate([mixes[p, slot, 0], mixes[p, slot, 1]], axis=0)
            left = dot(mixed, volts[0, p, channel])
            right = dot(mixed, volts[1, p, channel])
            reals.append(left[:beams] - right[beams:])
            imags.append(left[beams:] + right[:beams])
        share = beams // groups
        return [
            jnp.concatenate([part[g * share : (g + 1) * share] for part in reals + imags], axis=0)
            for g in range(groups)
        ]

    def near_copies(i):
        return [
            remote(away_code.at[i], near_code.at[i], near_send.at[0, i], near_recv.at[0, i], partner),
            remote(away_step.at[i], near_step.at[i], near_send.at[1, i], near_recv.at[1, i], partner),
        ]

    @pl.loop(0, fars)
    def _(i):
        there = far_of(i)
        pass_on(2 * there + side)
        for g, rows in enumerate(partial(2 * there + 1 - side)):
            away_code[i, g], away_step[i, g] = encode(rows)
        for copy in near_copies(i):
            copy.start()

    def sum_copies(i, g, target, source):
        device = (2 * target + side, g)
        return [
            remote(sum_code.at[i, g], code_out.at[source], sum_send.at[0, i * groups + g], sum_recv.at[0, source], device),
            remote(sum_step.at[i, g], step_out.at[source], sum_send.at[1, i * groups + g], sum_recv.at[1, source], device),
        ]

    origin = far * groups + group

    @pl.loop(0, fars)
    def _(i):
        there = far_of(i)
        parts = partial(2 * there + side)
        for copy in near_copies(i):
            copy.wait_recv()
        for g, rows in enumerate(parts):
            sum_code[i, g], sum_step[i, g] = encode(rows + decode(near_code[i, g], near_step[i, g]))

            @pl.when((there != far) | (g != group))
            def _(g=g):
                for copy in sum_copies(i, g, there, origin):
                    copy.start()

    last = fars - 1
    kept = [
        pltpu.make_async_copy(sum_code.at[last, group], code_out.at[origin], own.at[0]),
        pltpu.make_async_copy(sum_step.at[last, group], step_out.at[origin], own.at[1]),
    ]
    for copy in kept:
        copy.start()

    @pl.loop(0, chans)
    def _(slot):
        @pl.when(slot != chan)
        def _():
            weight_copy(slot, slot).wait_send()
            pass_copy(half, slot).wait_send()

    @pl.loop(0, fars)
    def _(i):
        for copy in near_copies(i):
            copy.wait_send()
        there = far_of(i)
        for g in range(groups):
            @pl.when((there != far) | (g != group))
            def _(g=g):
                for copy in sum_copies(i, g, there, there * groups + g):
                    copy.wait_send()
                    copy.wait_recv()

    for copy in kept:
        copy.wait()


def form_sums(voltages, weights, channel_map, chans, groups):
    parts, pols, channels, antennas, times = voltages.shape
    beams = weights.shape[2]
    sliced = antennas % 128 == 0
    if not sliced:
        weights = weights.reshape(2, pols, beams, chans, antennas).transpose(3, 0, 1, 2, 4)
    rows = 2 * pols * beams // groups
    fars = chans // 2
    any_spec = pl.BlockSpec(memory_space=pl.ANY)
    code, step = (fars, groups, rows, times), (fars, groups, 1, times)
    dma = pltpu.SemaphoreType.DMA
    return pl.pallas_call(
        functools.partial(form_kernel, chans, groups, sliced),
        in_specs=[pl.BlockSpec(memory_space=pltpu.SMEM), any_spec, any_spec],
        out_specs=[any_spec, any_spec],
        out_shape=[
            jax.ShapeDtypeStruct((fars * groups, rows, times), jnp.int16),
            jax.ShapeDtypeStruct((fars * groups, 1, times), jnp.float32),
        ],
        scratch_shapes=[
            pltpu.VMEM(voltages.shape, voltages.dtype),
            pltpu.VMEM((pols, chans, 2, beams, antennas), weights.dtype),
        ]
        + [pltpu.VMEM(code, jnp.int16), pltpu.VMEM(step, jnp.float32)] * 3
        + [
            dma((pols + 1,)), dma((chans,)), dma((chans,)), dma((chans,)), dma((chans,)),
            dma((2, fars)), dma((2, fars)), dma((2, fars * groups)), dma((2, fars * groups)),
        ],
        compiler_params=pltpu.CompilerParams(collective_id=0, has_side_effects=True, vmem_limit_bytes=48 << 20),
        name="form_sums",
    )(channel_map, voltages, weights)


def split(value):
    high = value.astype(jnp.bfloat16)
    return high, (value - high.astype(jnp.float32)).astype(jnp.bfloat16)


def transform(value, high, low):
    rows = value.shape[0]
    first, second = split(value)
    both = dot(jnp.concatenate([first, second], axis=0), high)
    return both[:rows] + both[rows:] + dot(first, low)


def dedisperse_kernel(chans, groups, code_ref, step_ref, resp_ref, table_ref, out_ref, sums):
    longest, beams = resp_ref.shape[2], resp_ref.shape[1]
    rows, times = code_ref.shape[1], code_ref.shape[2]
    half = rows // 2
    for g in range(groups):

        def add(c, total, g=g):
            at = c * groups + g
            return total + decode(code_ref[at], step_ref[at])

        sums[g] = lax.fori_loop(0, chans, add, jnp.zeros((rows, times), jnp.float32))
    cos_high, cos_low, sin_high, sin_low = (table_ref[n] for n in range(4))
    resp = jnp.concatenate([resp_ref[0], resp_ref[1]], axis=0)
    by_cos = transform(resp, cos_high[:longest], cos_low[:longest])
    by_sin = transform(resp, sin_high[:longest], sin_low[:longest])
    gain_real = (by_cos[:beams] + by_sin[beams:])[None]
    gain_imag = (by_cos[beams:] - by_sin[:beams])[None]

    per = times // longest
    count = groups * per
    blocks = []
    for r in range(2):
        pieces = [jnp.zeros((half, longest), jnp.float32)]
        for m in range(count):
            pieces.append(sums[m // per, r * half : (r + 1) * half, (m % per) * longest : (m % per + 1) * longest])
        blocks += [jnp.concatenate([pieces[m], pieces[m + 1]], axis=1) for m in range(count)]
    stacked = jnp.concatenate(blocks, axis=0)
    size = count * half
    by_cos = transform(stacked, cos_high, cos_low)
    by_sin = transform(stacked, sin_high, sin_low)
    shape = (size // beams, beams, 2 * longest)
    spec_real = (by_cos[:size] + by_sin[size:]).reshape(shape)
    spec_imag = (by_cos[size:] - by_sin[:size]).reshape(shape)
    prod_real = (spec_real * gain_real - spec_imag * gain_imag).reshape(size, 2 * longest)
    prod_imag = (spec_real * gain_imag + spec_imag * gain_real).reshape(size, 2 * longest)
    stacked = jnp.concatenate([prod_real, prod_imag], axis=0) * (0.5 / longest)
    by_cos = transform(stacked, cos_high[:, longest:], cos_low[:, longest:])
    by_sin = transform(stacked, sin_high[:, longest:], sin_low[:, longest:])
    results = (by_cos[:size] - by_sin[size:], by_cos[size:] + by_sin[:size])
    for r in range(2):
        for m in range(count):
            for p in range(half // beams):
                start = m * half + p * beams
                out_ref[0, r, p, :, m * longest : (m + 1) * longest] = results[r][start : start + beams]


def dedisperse(codes, steps, resp, chans, groups):
    rows, times = codes.shape[1:]
    beams, longest = resp.shape[1:]
    return pl.pallas_call(
        functools.partial(dedisperse_kernel, chans, groups),
        in_specs=[pl.BlockSpec(memory_space=pltpu.VMEM)] * 4,
        out_specs=pl.BlockSpec(memory_space=pltpu.VMEM),
        out_shape=jax.ShapeDtypeStruct((1, 2, rows // (2 * beams), beams, groups * times), jnp.float32),
        scratch_shapes=[pltpu.VMEM((groups, rows, times), jnp.float32)],
        compiler_params=pltpu.CompilerParams(vmem_limit_bytes=40 << 20),
        name="dedisperse",
    )(codes, steps, resp, jnp.asarray(fourier_tables(2 * longest)))


def on_device(chans, groups, voltages, weights, channel_map, sweep_response_taps, chirp_length):
    longest = sweep_response_taps.shape[3]
    lag = jnp.arange(longest, dtype=jnp.int32)
    inside = lag[None, :] < chirp_length[:, None]
    factor = lax.rsqrt(chirp_length.astype(jnp.float32))[:, None]
    resp = jnp.where(inside, sweep_response_taps[0], 0.0) * factor
    codes, steps = form_sums(voltages, weights[0], channel_map, chans, groups)
    return dedisperse(codes, steps, resp, chans // 2, groups)


def solution(mesh):
    return jax.shard_map(
        functools.partial(on_device, mesh.shape["chan"], mesh.shape["tm"]),
        mesh=mesh,
        in_specs=(
            P(None, None, None, "chan", "tm"),
            P("chan", None, None, None, None),
            P(),
            P("chan", None, "tm", None),
            P("tm"),
        ),
        out_specs=P("chan", None, None, "tm", None),
        check_vma=False,
    )
```

```python
import functools
import math

import jax
import jax.numpy as jnp
import ml_dtypes
import numpy as np
from jax import lax
from jax.experimental import pallas as pl
from jax.experimental.pallas import tpu as pltpu
from jax.sharding import PartitionSpec as P

TOP = 32767.0
MESH = pl.DeviceIdType.MESH


def dot(left, right):
    return jnp.dot(left, right, preferred_element_type=jnp.float32)


def fourier_tables(extent):
    counter = np.arange(extent, dtype=np.int64)
    angle = (counter[:, None] * counter[None, :] % extent) * (2.0 * math.pi / extent)
    tables = []
    for table in (np.cos(angle), np.sin(angle)):
        high = table.astype(ml_dtypes.bfloat16)
        low = (table - high.astype(np.float64)).astype(ml_dtypes.bfloat16)
        tables += [high, low]
    return np.stack(tables)


def encode(rows):
    peak = jnp.maximum(jnp.max(jnp.abs(rows), axis=0, keepdims=True), 1e-30)
    codes = jnp.round(rows * (TOP / peak)).astype(jnp.int32).astype(jnp.int16)
    return codes, peak * (1.0 / TOP)


def decode(codes, step):
    return codes.astype(jnp.int32).astype(jnp.float32) * step


def split(value):
    high = value.astype(jnp.bfloat16)
    return high, (value - high.astype(jnp.float32)).astype(jnp.bfloat16)


def transform(value, high, low):
    rows = value.shape[0]
    first, second = split(value)
    both = dot(jnp.concatenate([first, second], axis=0), high)
    return both[:rows] + both[rows:] + dot(first, low)


def gains(chirp_ref, taps_ref, table_ref):
    beams, longest = taps_ref.shape[2], taps_ref.shape[3]
    row = lax.broadcasted_iota(jnp.int32, (beams, longest), 0)
    lag = lax.broadcasted_iota(jnp.int32, (beams, longest), 1)
    length = jnp.zeros((beams, longest), jnp.int32)
    for b in range(beams):
        length = jnp.where(row == b, chirp_ref[b], length)
    factor = 1.0 / jnp.sqrt(length.astype(jnp.float32))
    resp = jnp.concatenate([jnp.where(lag < length, taps_ref[0, r], 0.0) * factor for r in range(2)], axis=0)
    by_cos = transform(resp, table_ref[0, :longest], table_ref[1, :longest])
    by_sin = transform(resp, table_ref[2, :longest], table_ref[3, :longest])
    return by_cos[:beams] + by_sin[beams:], by_cos[beams:] - by_sin[:beams]


def dedisperse(sums, gain_real, gain_imag, table_ref, out_ref):
    groups, rows, times = sums.shape
    beams, longest = gain_real.shape[1], gain_real.shape[2] // 2
    half = rows // 2
    cos_high, cos_low, sin_high, sin_low = (table_ref[n] for n in range(4))
    per = times // longest
    count = groups * per
    blocks = []
    for r in range(2):
        pieces = [jnp.zeros((half, longest), jnp.float32)]
        for m in range(count):
            pieces.append(sums[m // per, r * half : (r + 1) * half, (m % per) * longest : (m % per + 1) * longest])
        blocks += [jnp.concatenate([pieces[m], pieces[m + 1]], axis=1) for m in range(count)]
    stacked = jnp.concatenate(blocks, axis=0)
    size = count * half
    by_cos = transform(stacked, cos_high, cos_low)
    by_sin = transform(stacked, sin_high, sin_low)
    shape = (size // beams, beams, 2 * longest)
    spec_real = (by_cos[:size] + by_sin[size:]).reshape(shape)
    spec_imag = (by_cos[size:] - by_sin[:size]).reshape(shape)
    prod_real = (spec_real * gain_real - spec_imag * gain_imag).reshape(size, 2 * longest)
    prod_imag = (spec_real * gain_imag + spec_imag * gain_real).reshape(size, 2 * longest)
    stacked = jnp.concatenate([prod_real, prod_imag], axis=0) * (0.5 / longest)
    by_cos = transform(stacked, cos_high[:, longest:], cos_low[:, longest:])
    by_sin = transform(stacked, sin_high[:, longest:], sin_low[:, longest:])
    results = (by_cos[:size] - by_sin[size:], by_cos[size:] + by_sin[:size])
    for r in range(2):
        for m in range(count):
            for p in range(half // beams):
                start = m * half + p * beams
                out_ref[0, r, p, :, m * longest : (m + 1) * longest] = results[r][start : start + beams]


def form_kernel(
    chans, groups, sliced, map_ref, chirp_ref, volt_ref, weight_ref, table_hbm, taps_ref, out_ref,
    volts, mixes, tables, code_out, step_out, gain, sums, away_code, away_step, near_code, near_step, sum_code, sum_step,
    own, weight_send, weight_recv, pass_send, pass_recv, near_send, near_recv, sum_send, sum_recv,
):
    pols, beams, antennas = mixes.shape[0], mixes.shape[3], mixes.shape[4]
    chan, group = lax.axis_index("chan"), lax.axis_index("tm")
    far, side = lax.div(chan, 2), lax.rem(chan, 2)
    fars = chans // 2
    half = lax.rem(group, 2)
    sibling = (chan, group + 1 - 2 * half)
    partner = (chan + 1 - 2 * side, group)
    total = chans * groups
    me = chan * groups + group
    barrier = pltpu.get_barrier_semaphore()
    table_load = pltpu.make_async_copy(table_hbm, tables, own.at[pols + 1])
    table_load.start()
    load = pltpu.make_async_copy(volt_ref, volts, own.at[pols])
    load.start()

    @pl.loop(1, total)
    def _(k):
        other = lax.rem(me + k, total)
        device = (lax.div(other, groups), lax.rem(other, groups))
        pl.semaphore_signal(barrier, inc=1, device_id=device, device_id_type=MESH)

    def piece(p, target):
        if sliced:
            return weight_ref.at[:, p, :, pl.ds(pl.multiple_of(target * antennas, antennas), antennas)]
        return weight_ref.at[target, :, p]

    mine = [pltpu.make_async_copy(piece(p, chan), mixes.at[p, chan], own.at[p]) for p in range(pols)]
    for copy in mine:
        copy.start()
    pl.semaphore_wait(barrier, total - 1)

    def remote(source, target, send, recv, device):
        return pltpu.make_async_remote_copy(
            src_ref=source, dst_ref=target, send_sem=send, recv_sem=recv, device_id=device, device_id_type=MESH
        )

    def weight_copy(target, slot):
        return remote(piece(half, target), mixes.at[half, slot], weight_send.at[target], weight_recv.at[slot], (target, group))

    def pass_copy(p, slot):
        return remote(mixes.at[p, slot], mixes.at[p, slot], pass_send.at[slot], pass_recv.at[slot], sibling)

    @pl.loop(0, fars)
    def _(i):
        weight_copy(2 * lax.rem(far + fars - 1 - i, fars) + 1 - side, chan).start()

    @pl.loop(0, fars - 1)
    def _(i):
        weight_copy(2 * lax.rem(far + fars - 1 - i, fars) + side, chan).start()

    table_load.wait()
    gain[0], gain[1] = gains(chirp_ref, taps_ref, tables)
    for copy in mine:
        copy.wait()

    def far_of(i):
        return lax.rem(far + i + 1, fars)

    def pass_on(slot):
        @pl.when(slot != chan)
        def _():
            weight_copy(slot, slot).wait_recv()
            pass_copy(half, slot).start()

    def turn(i):
        there = far_of(lax.rem(i, fars))
        return 2 * there + jnp.where(i < fars, 1 - side, side)

    pass_on(turn(0))
    load.wait()

    def partial(slot):
        @pl.when(slot != chan)
        def _():
            pass_copy(1 - half, slot).wait_recv()

        channel = map_ref[slot]
        reals, imags = [], []
        for p in range(pols):
            mixed = jnp.concatenate([mixes[p, slot, 0], mixes[p, slot, 1]], axis=0)
            left = dot(mixed, volts[0, p, channel])
            right = dot(mixed, volts[1, p, channel])
            reals.append(left[:beams] - right[beams:])
            imags.append(left[beams:] + right[:beams])
        share = beams // groups
        return [
            jnp.concatenate([part[g * share : (g + 1) * share] for part in reals + imags], axis=0)
            for g in range(groups)
        ]

    def near_copies(i):
        return [
            remote(away_code.at[i], near_code.at[i], near_send.at[0, i], near_recv.at[0, i], partner),
            remote(away_step.at[i], near_step.at[i], near_send.at[1, i], near_recv.at[1, i], partner),
        ]

    @pl.loop(0, fars)
    def _(i):
        there = far_of(i)
        pass_on(turn(i + 1))
        for g, rows in enumerate(partial(2 * there + 1 - side)):
            away_code[i, g], away_step[i, g] = encode(rows)
        for copy in near_copies(i):
            copy.start()

    def sum_copies(i, g, target, source):
        device = (2 * target + side, g)
        return [
            remote(sum_code.at[i, g], code_out.at[source], sum_send.at[0, i * groups + g], sum_recv.at[0, source], device),
            remote(sum_step.at[i, g], step_out.at[source], sum_send.at[1, i * groups + g], sum_recv.at[1, source], device),
        ]

    origin = far * groups + group

    @pl.loop(0, fars)
    def _(i):
        there = far_of(i)

        @pl.when(i < fars - 1)
        def _():
            pass_on(turn(fars + i + 1))

        parts = partial(2 * there + side)
        for copy in near_copies(i):
            copy.wait_recv()
        for g, rows in enumerate(parts):
            sum_code[i, g], sum_step[i, g] = encode(rows + decode(near_code[i, g], near_step[i, g]))

            @pl.when((there != far) | (g != group))
            def _(g=g):
                for copy in sum_copies(i, g, there, origin):
                    copy.start()

    last = fars - 1
    kept = [
        pltpu.make_async_copy(sum_code.at[last, group], code_out.at[origin], own.at[0]),
        pltpu.make_async_copy(sum_step.at[last, group], step_out.at[origin], own.at[1]),
    ]
    for copy in kept:
        copy.start()

    for copy in kept:
        copy.wait()
    sums[...] = jnp.zeros(sums.shape, sums.dtype)

    @pl.loop(0, fars)
    def _(i):
        there = lax.rem(far + fars - 1 - i, fars)
        for g in range(groups):
            at = there * groups + g

            @pl.when((there != far) | (g != group))
            def _(at=at, g=g):
                for copy in sum_copies(0, g, there, at):
                    copy.wait_recv()

            sums[g] += decode(code_out[at], step_out[at])

    dedisperse(sums, gain[0:1], gain[1:2], tables, out_ref)

    @pl.loop(0, chans)
    def _(slot):
        @pl.when(slot != chan)
        def _():
            weight_copy(slot, slot).wait_send()
            pass_copy(half, slot).wait_send()

    @pl.loop(0, fars)
    def _(i):
        for copy in near_copies(i):
            copy.wait_send()
        there = far_of(i)
        for g in range(groups):
            @pl.when((there != far) | (g != group))
            def _(g=g):
                for copy in sum_copies(i, g, there, origin):
                    copy.wait_send()


def form_series(voltages, weights, channel_map, taps, chirp_length, chans, groups):
    parts, pols, channels, antennas, times = voltages.shape
    beams = weights.shape[2]
    sliced = antennas % 128 == 0
    if not sliced:
        weights = weights.reshape(2, pols, beams, chans, antennas).transpose(3, 0, 1, 2, 4)
    rows, share, longest = 2 * pols * beams // groups, beams // groups, taps.shape[3]
    fars = chans // 2
    table = jnp.asarray(fourier_tables(2 * longest))
    any_spec = pl.BlockSpec(memory_space=pl.ANY)
    code, step = (fars, groups, rows, times), (fars, groups, 1, times)
    dma = pltpu.SemaphoreType.DMA
    return pl.pallas_call(
        functools.partial(form_kernel, chans, groups, sliced),
        in_specs=[pl.BlockSpec(memory_space=pltpu.SMEM)] * 2 + [any_spec] * 3 + [pl.BlockSpec(memory_space=pltpu.VMEM)],
        out_specs=pl.BlockSpec(memory_space=pltpu.VMEM),
        out_shape=jax.ShapeDtypeStruct((1, 2, pols, share, groups * times), jnp.float32),
        scratch_shapes=[
            pltpu.VMEM(voltages.shape, voltages.dtype),
            pltpu.VMEM((pols, chans, 2, beams, antennas), weights.dtype),
            pltpu.VMEM(table.shape, table.dtype),
            pltpu.VMEM((fars * groups, rows, times), jnp.int16),
            pltpu.VMEM((fars * groups, 1, times), jnp.float32),
            pltpu.VMEM((2, share, 2 * longest), jnp.float32),
            pltpu.VMEM((groups, rows, times), jnp.float32),
        ]
        + [pltpu.VMEM(code, jnp.int16), pltpu.VMEM(step, jnp.float32)] * 3
        + [
            dma((pols + 2,)), dma((chans,)), dma((chans,)), dma((chans,)), dma((chans,)),
            dma((2, fars)), dma((2, fars)), dma((2, fars * groups)), dma((2, fars * groups)),
        ],
        compiler_params=pltpu.CompilerParams(collective_id=0, has_side_effects=True, vmem_limit_bytes=56 << 20),
        name="form_series",
    )(channel_map, chirp_length, voltages, weights, table, taps)


def on_device(chans, groups, voltages, weights, channel_map, sweep_response_taps, chirp_length):
    return form_series(voltages, weights[0], channel_map, sweep_response_taps, chirp_length, chans, groups)


def solution(mesh):
    return jax.shard_map(
        functools.partial(on_device, mesh.shape["chan"], mesh.shape["tm"]),
        mesh=mesh,
        in_specs=(
            P(None, None, None, "chan", "tm"),
            P("chan", None, None, None, None),
            P(),
            P("chan", None, "tm", None),
            P("tm"),
        ),
        out_specs=P("chan", None, None, "tm", None),
        check_vma=False,
    )
```

```python
import functools
import math

import jax
import jax.numpy as jnp
import ml_dtypes
import numpy as np
from jax import lax
from jax.experimental import pallas as pl
from jax.experimental.pallas import tpu as pltpu
from jax.sharding import PartitionSpec as P

TOP = 32767.0
MESH = pl.DeviceIdType.MESH


def dot(left, right):
    return jnp.dot(left, right, preferred_element_type=jnp.float32)


def fourier_tables(extent):
    counter = np.arange(extent, dtype=np.int64)
    angle = (counter[:, None] * counter[None, :] % extent) * (2.0 * math.pi / extent)
    tables = []
    for table in (np.cos(angle), np.sin(angle)):
        high = table.astype(ml_dtypes.bfloat16)
        low = (table - high.astype(np.float64)).astype(ml_dtypes.bfloat16)
        tables += [high, low]
    return np.stack(tables)


def peak_of(rows):
    return jnp.maximum(jnp.max(jnp.abs(rows), axis=0, keepdims=True), 1e-30)


def encode(rows, peak):
    codes = jnp.round(rows * (TOP / peak)).astype(jnp.int32).astype(jnp.int16)
    return codes, peak * (1.0 / TOP)


def decode(codes, step):
    return codes.astype(jnp.int32).astype(jnp.float32) * step


def split(value):
    high = value.astype(jnp.bfloat16)
    return high, (value - high.astype(jnp.float32)).astype(jnp.bfloat16)


def transform(value, high, low):
    rows = value.shape[0]
    first, second = split(value)
    both = dot(jnp.concatenate([first, second], axis=0), high)
    return both[:rows] + both[rows:] + dot(first, low)


def gains(chirp_ref, taps_ref, table_ref):
    beams, longest = taps_ref.shape[2], taps_ref.shape[3]
    row = lax.broadcasted_iota(jnp.int32, (beams, longest), 0)
    lag = lax.broadcasted_iota(jnp.int32, (beams, longest), 1)
    length = jnp.zeros((beams, longest), jnp.int32)
    for b in range(beams):
        length = jnp.where(row == b, chirp_ref[b], length)
    factor = 1.0 / jnp.sqrt(length.astype(jnp.float32))
    resp = jnp.concatenate([jnp.where(lag < length, taps_ref[0, r], 0.0) * factor for r in range(2)], axis=0)
    by_cos = transform(resp, table_ref[0, :longest], table_ref[1, :longest])
    by_sin = transform(resp, table_ref[2, :longest], table_ref[3, :longest])
    return by_cos[:beams] + by_sin[beams:], by_cos[beams:] - by_sin[:beams]


def dedisperse(sums, gain_real, gain_imag, table_ref, out_ref):
    groups, rows, times = sums.shape
    beams, longest = gain_real.shape[1], gain_real.shape[2] // 2
    half = rows // 2
    cos_high, cos_low, sin_high, sin_low = (table_ref[n] for n in range(4))
    per = times // longest
    count = groups * per
    blocks = []
    for r in range(2):
        pieces = [jnp.zeros((half, longest), jnp.float32)]
        for m in range(count):
            pieces.append(sums[m // per, r * half : (r + 1) * half, (m % per) * longest : (m % per + 1) * longest])
        blocks += [jnp.concatenate([pieces[m], pieces[m + 1]], axis=1) for m in range(count)]
    stacked = jnp.concatenate(blocks, axis=0)
    size = count * half
    by_cos = transform(stacked, cos_high, cos_low)
    by_sin = transform(stacked, sin_high, sin_low)
    shape = (size // beams, beams, 2 * longest)
    spec_real = (by_cos[:size] + by_sin[size:]).reshape(shape)
    spec_imag = (by_cos[size:] - by_sin[:size]).reshape(shape)
    prod_real = (spec_real * gain_real - spec_imag * gain_imag).reshape(size, 2 * longest)
    prod_imag = (spec_real * gain_imag + spec_imag * gain_real).reshape(size, 2 * longest)
    stacked = jnp.concatenate([prod_real, prod_imag], axis=0) * (0.5 / longest)
    by_cos = transform(stacked, cos_high[:, longest:], cos_low[:, longest:])
    by_sin = transform(stacked, sin_high[:, longest:], sin_low[:, longest:])
    results = (by_cos[:size] - by_sin[size:], by_cos[size:] + by_sin[:size])
    for r in range(2):
        for m in range(count):
            for p in range(half // beams):
                start = m * half + p * beams
                out_ref[0, r, p, :, m * longest : (m + 1) * longest] = results[r][start : start + beams]


def form_kernel(
    chans, groups, sliced, map_ref, chirp_ref, volt_ref, weight_ref, table_hbm, taps_ref, out_ref,
    volts, mixes, tables, code_out, step_out, gain, sums, away_code, away_step, near_code, near_step, sum_code, sum_step,
    own, weight_send, weight_recv, pass_send, pass_recv, near_send, near_recv, sum_send, sum_recv,
):
    pols, beams, antennas = mixes.shape[0], mixes.shape[3], mixes.shape[4]
    chan, group = lax.axis_index("chan"), lax.axis_index("tm")
    far, side = lax.div(chan, 2), lax.rem(chan, 2)
    fars = chans // 2
    half = lax.rem(group, 2)
    sibling = (chan, group + 1 - 2 * half)
    partner = (chan + 1 - 2 * side, group)
    barrier = pltpu.get_barrier_semaphore()
    table_load = pltpu.make_async_copy(table_hbm, tables, own.at[pols + 1])
    table_load.start()
    load = pltpu.make_async_copy(volt_ref, volts, own.at[pols])
    load.start()

    @pl.loop(1, chans)
    def _(k):
        pl.semaphore_signal(barrier, inc=1, device_id=(lax.rem(chan + k, chans), group), device_id_type=MESH)

    @pl.loop(0, fars)
    def _(k):
        for d in range(1, groups):
            device = (2 * lax.rem(far + k, fars) + side, lax.rem(group + d, groups))
            pl.semaphore_signal(barrier, inc=1, device_id=device, device_id_type=MESH)

    def piece(p, target):
        if sliced:
            return weight_ref.at[:, p, :, pl.ds(pl.multiple_of(target * antennas, antennas), antennas)]
        return weight_ref.at[target, :, p]

    mine = [pltpu.make_async_copy(piece(p, chan), mixes.at[p, chan], own.at[p]) for p in range(pols)]
    for copy in mine:
        copy.start()
    table_load.wait()
    gain[0], gain[1] = gains(chirp_ref, taps_ref, tables)
    pl.semaphore_wait(barrier, chans - 1 + fars * (groups - 1))

    def remote(source, target, send, recv, device):
        return pltpu.make_async_remote_copy(
            src_ref=source, dst_ref=target, send_sem=send, recv_sem=recv, device_id=device, device_id_type=MESH
        )

    def weight_copy(target, slot):
        return remote(piece(half, target), mixes.at[half, slot], weight_send.at[target], weight_recv.at[slot], (target, group))

    def pass_copy(p, slot):
        return remote(mixes.at[p, slot], mixes.at[p, slot], pass_send.at[slot], pass_recv.at[slot], sibling)

    @pl.loop(0, fars)
    def _(i):
        weight_copy(2 * lax.rem(far + fars - 1 - i, fars) + 1 - side, chan).start()

    @pl.loop(0, fars - 1)
    def _(i):
        weight_copy(2 * lax.rem(far + fars - 1 - i, fars) + side, chan).start()

    for copy in mine:
        copy.wait()

    def far_of(i):
        return lax.rem(far + i + 1, fars)

    def pass_on(slot):
        @pl.when(slot != chan)
        def _():
            weight_copy(slot, slot).wait_recv()
            pass_copy(half, slot).start()

    def turn(i):
        there = far_of(lax.rem(i, fars))
        return 2 * there + jnp.where(i < fars, 1 - side, side)

    pass_on(turn(0))
    load.wait()

    def partial(slot):
        @pl.when(slot != chan)
        def _():
            pass_copy(1 - half, slot).wait_recv()

        channel = map_ref[slot]
        reals, imags = [], []
        for p in range(pols):
            mixed = jnp.concatenate([mixes[p, slot, 0], mixes[p, slot, 1]], axis=0)
            left = dot(mixed, volts[0, p, channel])
            right = dot(mixed, volts[1, p, channel])
            reals.append(left[:beams] - right[beams:])
            imags.append(left[beams:] + right[:beams])
        share = beams // groups
        return [
            jnp.concatenate([part[g * share : (g + 1) * share] for part in reals + imags], axis=0)
            for g in range(groups)
        ]

    def near_copies(i):
        return [
            remote(away_code.at[i], near_code.at[i], near_send.at[0, i], near_recv.at[0, i], partner),
            remote(away_step.at[i], near_step.at[i], near_send.at[1, i], near_recv.at[1, i], partner),
        ]

    @pl.loop(0, fars)
    def _(i):
        there = far_of(i)
        pass_on(turn(i + 1))
        parts = partial(2 * there + 1 - side)
        peak = functools.reduce(jnp.maximum, [peak_of(rows) for rows in parts])
        for g, rows in enumerate(parts):
            away_code[i, g], away_step[i] = encode(rows, peak)
        for copy in near_copies(i):
            copy.start()

    def sum_copies(i, g, target, source):
        device = (2 * target + side, g)
        return [
            remote(sum_code.at[i, g], code_out.at[source], sum_send.at[0, i * groups + g], sum_recv.at[0, source], device),
            remote(sum_step.at[i, g], step_out.at[source], sum_send.at[1, i * groups + g], sum_recv.at[1, source], device),
        ]

    origin = far * groups + group

    @pl.loop(0, fars)
    def _(i):
        there = far_of(i)

        @pl.when(i < fars - 1)
        def _():
            pass_on(turn(fars + i + 1))

        parts = partial(2 * there + side)
        for copy in near_copies(i):
            copy.wait_recv()
        for g, rows in enumerate(parts):
            rows += decode(near_code[i, g], near_step[i])
            sum_code[i, g], sum_step[i, g] = encode(rows, peak_of(rows))

            @pl.when((there != far) | (g != group))
            def _(g=g):
                for copy in sum_copies(i, g, there, origin):
                    copy.start()

    last = fars - 1
    kept = [
        pltpu.make_async_copy(sum_code.at[last, group], code_out.at[origin], own.at[0]),
        pltpu.make_async_copy(sum_step.at[last, group], step_out.at[origin], own.at[1]),
    ]
    for copy in kept:
        copy.start()

    for copy in kept:
        copy.wait()
    sums[...] = jnp.zeros(sums.shape, sums.dtype)

    @pl.loop(0, fars)
    def _(i):
        there = lax.rem(far + fars - 1 - i, fars)
        for g in range(groups):
            at = there * groups + g

            @pl.when((there != far) | (g != group))
            def _(at=at, g=g):
                for copy in sum_copies(0, g, there, at):
                    copy.wait_recv()

            sums[g] += decode(code_out[at], step_out[at])

    dedisperse(sums, gain[0:1], gain[1:2], tables, out_ref)

    @pl.loop(0, chans)
    def _(slot):
        @pl.when(slot != chan)
        def _():
            weight_copy(slot, slot).wait_send()
            pass_copy(half, slot).wait_send()

    @pl.loop(0, fars)
    def _(i):
        for copy in near_copies(i):
            copy.wait_send()
        there = far_of(i)
        for g in range(groups):
            @pl.when((there != far) | (g != group))
            def _(g=g):
                for copy in sum_copies(i, g, there, origin):
                    copy.wait_send()


def form_series(voltages, weights, channel_map, taps, chirp_length, chans, groups):
    parts, pols, channels, antennas, times = voltages.shape
    beams = weights.shape[2]
    sliced = antennas % 128 == 0
    if not sliced:
        weights = weights.reshape(2, pols, beams, chans, antennas).transpose(3, 0, 1, 2, 4)
    rows, share, longest = 2 * pols * beams // groups, beams // groups, taps.shape[3]
    fars = chans // 2
    table = jnp.asarray(fourier_tables(2 * longest))
    any_spec = pl.BlockSpec(memory_space=pl.ANY)
    code, step = (fars, groups, rows, times), (fars, groups, 1, times)
    dma = pltpu.SemaphoreType.DMA
    return pl.pallas_call(
        functools.partial(form_kernel, chans, groups, sliced),
        in_specs=[pl.BlockSpec(memory_space=pltpu.SMEM)] * 2 + [any_spec] * 3 + [pl.BlockSpec(memory_space=pltpu.VMEM)],
        out_specs=pl.BlockSpec(memory_space=pltpu.VMEM),
        out_shape=jax.ShapeDtypeStruct((1, 2, pols, share, groups * times), jnp.float32),
        scratch_shapes=[
            pltpu.VMEM(voltages.shape, voltages.dtype),
            pltpu.VMEM((pols, chans, 2, beams, antennas), weights.dtype),
            pltpu.VMEM(table.shape, table.dtype),
            pltpu.VMEM((fars * groups, rows, times), jnp.int16),
            pltpu.VMEM((fars * groups, 1, times), jnp.float32),
            pltpu.VMEM((2, share, 2 * longest), jnp.float32),
            pltpu.VMEM((groups, rows, times), jnp.float32),
        ]
        + [pltpu.VMEM(code, jnp.int16), pltpu.VMEM((fars, 1, times), jnp.float32)] * 2
        + [pltpu.VMEM(code, jnp.int16), pltpu.VMEM(step, jnp.float32)]
        + [
            dma((pols + 2,)), dma((chans,)), dma((chans,)), dma((chans,)), dma((chans,)),
            dma((2, fars)), dma((2, fars)), dma((2, fars * groups)), dma((2, fars * groups)),
        ],
        compiler_params=pltpu.CompilerParams(collective_id=0, has_side_effects=True, vmem_limit_bytes=56 << 20),
        name="form_series",
    )(channel_map, chirp_length, voltages, weights, table, taps)


def on_device(chans, groups, voltages, weights, channel_map, sweep_response_taps, chirp_length):
    return form_series(voltages, weights[0], channel_map, sweep_response_taps, chirp_length, chans, groups)


def solution(mesh):
    return jax.shard_map(
        functools.partial(on_device, mesh.shape["chan"], mesh.shape["tm"]),
        mesh=mesh,
        in_specs=(
            P(None, None, None, "chan", "tm"),
            P("chan", None, None, None, None),
            P(),
            P("chan", None, "tm", None),
            P("tm"),
        ),
        out_specs=P("chan", None, None, "tm", None),
        check_vma=False,
    )
```
